32 devices in a mesh: chan: 8 (over z, y), tm: 4 (over x, core).
Axes of the slice: x: 2, y: 2, z: 4, core: 2. Of those that a mesh axis runs over, the one named last changes fastest.
Arguments:
- samples: bfloat16 [1024, 2, 16, 16384], P('chan', None, 'tm'), may hold values from -6 to 6
- filter_taps: float32 [4, 16384], replicated, may hold values from -3 to 3
Outputs:
- visibility: float32 [8, 1024, 2048], P('chan', 'tm')
The draws below stay inside these ranges and needn't reach their ends.
All inputs are finite; a program needn't handle non-finite values.
Results may differ from the reference program's by a relative error of at most 0.01.
Values may be sent and summed in bfloat16 or wider, within the bound.
No kernel may reach another device: no remote copies, remote signals or barrier semaphores. Data moves between devices by JAX's collectives and lax.ppermute only.
A program may use at most 192 MiB of HBM per device.

```python
import math
import jax
import jax.numpy as jnp
from jax import lax

INPUTS = 1024
F = 16384
ROOT = 128
TAPS = 4
SPEC_DEV = 4
SPECTRA = 16
BINS = 8
BIN = 2048
N_TM = 4


def block_scale(rng, dims, shards, smallest, high):
    loudness, own = 1.0, jax.random.fold_in(rng, 6)
    for dim, blocks in shards:
        draws = jnp.exp(jax.random.uniform(jax.random.fold_in(own, dim), (blocks,), jnp.float32, smallest / len(shards), high / len(shards)))
        loudness = loudness * jnp.repeat(draws, dims[dim] // blocks).reshape([-1 if axis == dim else 1 for axis in range(len(dims))])
    return loudness


def centred(rng, extent, spread, most, cuts=(), kind=jnp.bfloat16):
    array = spread * jax.random.normal(rng, extent, jnp.float32)
    if cuts:
        array = array * block_scale(rng, extent, cuts, -0.22, 0.18)
    return jnp.clip(array, -most, most).astype(kind)


def setup_inputs(seed: int = 0) -> dict:
    key_of = jax.random.split(jax.random.key(seed), 3)
    samples = centred(key_of[0], (INPUTS, 2, SPECTRA, F), 1.0, 6.0, ((0, 8), (2, 4)))
    filter_taps = centred(key_of[1], (TAPS, F), 0.5, 3.0, (), jnp.float32)
    return dict(samples=samples, filter_taps=filter_taps)


def dft_tables(length):
    indices = jnp.arange(length, dtype=jnp.int32)
    product = (indices[:, None] * indices[None, :]) % length
    angles = product.astype(jnp.float32) * (2.0 * math.pi / length)
    cosine = jnp.cos(angles)
    sines_table = jnp.sin(angles)
    upper = jnp.stack([cosine, sines_table], axis=1)
    lower = jnp.stack([-sines_table, cosine], axis=1)
    return jnp.stack([upper, lower], axis=0).astype(jnp.bfloat16)


def channelize(window, filter_taps, number):
    filtered = filter_taps[0][None, None, None, :] * window[:, :, 0:number].astype(jnp.float32)
    for tap_index in range(1, TAPS):
        filtered = filtered + filter_taps[tap_index][None, None, None, :] * window[:, :, tap_index:tap_index + number].astype(jnp.float32)
    filtered = filtered.astype(jnp.bfloat16).reshape(window.shape[0], 2, number, ROOT, ROOT)
    matrix = dft_tables(ROOT)
    first_pass = jnp.einsum('pcra,irsab->ipscb', matrix.astype(jnp.float32), filtered.astype(jnp.float32))
    indices = jnp.arange(ROOT, dtype=jnp.int32)
    product = (indices[:, None] * indices[None, :]) % (ROOT * ROOT)
    angles = product.astype(jnp.float32) * (2.0 * math.pi / (ROOT * ROOT))
    cosine = jnp.cos(angles)
    sines_table = jnp.sin(angles)
    real_part = first_pass[:, 0]
    imag_part = first_pass[:, 1]
    twisted = jnp.stack([(real_part * cosine + imag_part * sines_table) / ROOT, (imag_part * cosine - real_part * sines_table) / ROOT], axis=1).astype(jnp.bfloat16)
    spectra = jnp.einsum('pdqb,iqscb->ipsdc', matrix.astype(jnp.float32), twisted.astype(jnp.float32))
    return spectra.astype(jnp.bfloat16)


def hermitian_operands(member):
    flattened = member.reshape(member.shape[0], -1)
    swapped = jnp.concatenate([-member[:, 1:2], member[:, 0:1]], axis=1).reshape(member.shape[0], -1)
    return flattened, jnp.concatenate([flattened, swapped], axis=0)


def correlate(row_side, col_side, factor):
    product = lax.dot_general(row_side.astype(jnp.float32), col_side.astype(jnp.float32), (((1,), (1,)), ((), ())))
    rounded = lax.optimization_barrier((product * factor).astype(jnp.bfloat16))
    return rounded.astype(jnp.float32)


def reference(samples, filter_taps):
    padded = jnp.concatenate([jnp.zeros((samples.shape[0], 2, TAPS - 1, F), jnp.bfloat16), samples], axis=2)

    def per_spectrum(position):
        window = lax.dynamic_slice_in_dim(padded, position, TAPS, 2)
        return channelize(window, filter_taps, 1)[:, :, 0]

    spectra = lax.map(per_spectrum, jnp.arange(SPECTRA, dtype=jnp.int32))
    per_bin = ROOT // BINS
    factor = 1.0 / (SPECTRA * BIN)

    def per_bin_fn(bin_index):
        chosen = lax.dynamic_slice_in_dim(spectra, bin_index * per_bin, per_bin, 3)
        total = jnp.zeros((INPUTS, 2 * INPUTS), jnp.float32)
        for time_block in range(N_TM):
            member = chosen[time_block * SPEC_DEV:(time_block + 1) * SPEC_DEV].transpose(1, 2, 0, 3, 4)
            row_side, col_side = hermitian_operands(member)
            total = total + correlate(row_side, col_side, factor)
        return total

    return lax.map(per_bin_fn, jnp.arange(BINS, dtype=jnp.int32))
```

```python
import functools
import math

import jax
import jax.numpy as jnp
import numpy as np
from jax import lax
from jax.experimental import pallas as pl
from jax.experimental.pallas import tpu as pltpu
from jax.sharding import PartitionSpec as P

ROOT = 128
TAPS = 4
GROUP = 16
TILE = 16
VMEM = 56 * 1024 * 1024


def tables():
    indices = np.arange(ROOT)
    product = np.outer(indices, indices)
    angles = (product % ROOT) * (2.0 * math.pi / ROOT)
    cosine, sine = np.cos(angles), np.sin(angles)
    matrix = np.block([[cosine, sine], [-sine, cosine]])
    angles = (product % ROOT**2) * (2.0 * math.pi / ROOT**2)
    twiddle = np.stack([np.cos(angles), np.sin(angles)]) / ROOT
    return jnp.asarray(matrix, jnp.bfloat16), jnp.asarray(twiddle, jnp.float32)


def dot_nt(rows, cols):
    return lax.dot_general(
        rows, cols, (((1,), (1,)), ((), ())), preferred_element_type=jnp.float32
    )


def channelize_kernel(number, bins, me_ref, own_ref, past_ref, taps_ref, matrix_ref, twiddle_ref,
                      *refs):
    out_refs, (frames, filtered, lines) = refs[:bins], refs[bins:]
    per = ROOT // bins
    which = pl.program_id(0)
    for part in range(2):
        for side, ref in enumerate((past_ref, own_ref)):
            frames[part, side] = ref[0, part].astype(jnp.float32)

    for first in range(0, ROOT, TILE):
        taps = [taps_ref[tap, pl.ds(first, TILE), :] for tap in range(TAPS)]
        for part in range(2):
            held = [
                frames[
                    part, f // number, pl.ds(first * number + f % number, TILE, stride=number), :
                ]
                for f in range(number - TAPS + 1, 2 * number)
            ]
            for s in range(number):
                total = taps[0] * held[s]
                for tap in range(1, TAPS):
                    total = total + taps[tap] * held[s + tap]
                filtered[pl.ds(part * ROOT + first, TILE), pl.ds(s * ROOT, ROOT)] = total.astype(
                    jnp.bfloat16
                )

    first_pass = jnp.dot(matrix_ref[...], filtered[...], preferred_element_type=jnp.float32)
    cosine, sine = twiddle_ref[0], twiddle_ref[1]
    twisted = []
    for s in range(number):
        real = first_pass[:ROOT, s * ROOT : (s + 1) * ROOT]
        imag = first_pass[ROOT:, s * ROOT : (s + 1) * ROOT]
        twisted.append(
            jnp.concatenate(
                [real * cosine + imag * sine, imag * cosine - real * sine], axis=1
            ).astype(jnp.bfloat16)
        )
    spectra = dot_nt(matrix_ref[...], jnp.concatenate(twisted, axis=0))
    for s in range(number):
        lines[pl.ds(s * 2 * ROOT * GROUP + which, 2 * ROOT, stride=GROUP), :] = spectra[
            :, s * ROOT : (s + 1) * ROOT
        ]

    @pl.when(which == GROUP - 1)
    def _():
        for k in range(bins):
            target = me_ref[0] ^ k

            def pack(step, _, k=k, target=target):
                line = step % per
                s, part = step // per // 2, step // per % 2
                row = ((s * 2 + part) * ROOT + target * per + line) * GROUP
                out_refs[k][0, part, s * per + line] = lines[
                    pl.ds(pl.multiple_of(row, GROUP), GROUP), :
                ].astype(jnp.bfloat16)
                return 0

            lax.fori_loop(0, number * 2 * per, pack, 0, unroll=8)


def channelize(me, samples, group, past, bins, taps, matrix, twiddle):
    number = samples.shape[2] // ROOT
    per = ROOT // bins
    work = GROUP * 2 * number * ROOT * ROOT
    block = (1, 2, number * per, GROUP, ROOT)
    return pl.pallas_call(
        functools.partial(channelize_kernel, number, bins),
        grid_spec=pltpu.PrefetchScalarGridSpec(
            num_scalar_prefetch=1,
            grid=(GROUP,),
            in_specs=[
                pl.BlockSpec(
                    (1, 2, ROOT * number, ROOT), lambda i, me: (group * GROUP + i, 0, 0, 0)
                ),
                pl.BlockSpec(
                    (1, 2, ROOT * number, ROOT), lambda i, me: (i, 0, 0, 0)
                ),
                pl.BlockSpec((TAPS, ROOT, ROOT), lambda i, me: (0, 0, 0)),
                pl.BlockSpec((2 * ROOT, 2 * ROOT), lambda i, me: (0, 0)),
                pl.BlockSpec((2, ROOT, ROOT), lambda i, me: (0, 0, 0)),
            ],
            out_specs=[pl.BlockSpec(block, lambda i, me: (0, 0, 0, 0, 0))] * bins,
            scratch_shapes=[
                pltpu.VMEM((2, 2, ROOT * number, ROOT), jnp.float32),
                pltpu.VMEM((2 * ROOT, number * ROOT), jnp.bfloat16),
                pltpu.VMEM((number * 2 * ROOT * GROUP, ROOT), jnp.float32),
            ],
        ),
        out_shape=[jax.ShapeDtypeStruct(block, jnp.bfloat16)] * bins,
        compiler_params=pltpu.CompilerParams(vmem_limit_bytes=VMEM),
        cost_estimate=pl.CostEstimate(
            flops=40 * ROOT * work, bytes_accessed=6 * work, transcendentals=0
        ),
        name="channelize",
    )(me, samples, past, taps, matrix, twiddle)


def correlate_kernel(bins, group, owners, factor, steps, me_ref, *refs):
    blocks, refs = refs[:bins], refs[bins:]
    if group:
        earlier_ref, refs = refs[0], refs[1:]
    kept_ref, out_ref, total = refs
    size = bins * GROUP
    deep = kept_ref.shape[1]
    step = pl.program_id(0)
    for k in range(bins):
        source = me_ref[0] ^ (bins - k if k else 0)
        kept_ref[:, :, pl.ds(pl.multiple_of(source * GROUP, GROUP), GROUP), :] = blocks[k][0]

    real, imag, negated = [], [], []
    for t in range(deep):
        a, b = kept_ref[0, t], kept_ref[1, t]
        real.append(jnp.concatenate([a, b], axis=1))
        imag.append(jnp.concatenate([-b, a], axis=1))
    here = jnp.concatenate(real, axis=1)
    cols = jnp.concatenate([here, jnp.concatenate(imag, axis=1)], axis=0)

    rows = here
    if group:
        earlier = [earlier_ref[part, t] for t in range(deep) for part in range(2)]
        rows = jnp.concatenate([jnp.concatenate(earlier, axis=1), here], axis=0)
    product = dot_nt(rows, cols)

    @pl.when(step == 0)
    def _():
        total[...] = product

    @pl.when(step > 0)
    def _():
        total[...] += product

    @pl.when(step == steps - 1)
    def _():
        share = size // owners
        for n in range(group + 1):
            tile = total[pl.ds(n * size, size), :] * factor
            for t in range(owners):
                out_ref[t, n] = tile[t * share : (t + 1) * share].astype(jnp.bfloat16)
            if n < group:
                mirror = jnp.concatenate([tile[:, :size].T, -tile[:, size:].T], axis=1)
                for t in range(owners):
                    out_ref[t, group + 1 + n] = mirror[t * share : (t + 1) * share].astype(
                        jnp.bfloat16
                    )


def correlate(me, blocks, kept, group, groups, owners, factor):
    bins = len(blocks)
    depth = blocks[0].shape[2]
    size = bins * GROUP
    deep = max(1, depth // 8)
    steps = depth // deep
    block_spec = pl.BlockSpec((1, 2, deep, GROUP, ROOT), lambda k, me: (0, 0, k, 0, 0))
    kept_shape = jax.ShapeDtypeStruct((2, depth, groups * size, ROOT), jnp.bfloat16)
    out_shape = jax.ShapeDtypeStruct(
        (owners, 2 * group + 1, size // owners, 2 * size), jnp.bfloat16
    )
    in_specs = [block_spec] * bins
    operands = list(blocks)
    aliases = {}
    if group:
        in_specs.append(
            pl.BlockSpec((2, deep, group * size, ROOT), lambda k, me: (0, k, 0, 0))
        )
        operands.append(kept)
        aliases = {1 + bins: 0}
    return pl.pallas_call(
        functools.partial(correlate_kernel, bins, group, owners, factor, steps),
        grid_spec=pltpu.PrefetchScalarGridSpec(
            num_scalar_prefetch=1,
            grid=(steps,),
            in_specs=in_specs,
            out_specs=[
                pl.BlockSpec((2, deep, size, ROOT), lambda k, me: (0, k, group, 0)),
                pl.BlockSpec(out_shape.shape, lambda k, me: (0, 0, 0, 0)),
            ],
            scratch_shapes=[pltpu.VMEM(((group + 1) * size, 2 * size), jnp.float32)],
        ),
        out_shape=[kept_shape, out_shape],
        input_output_aliases=aliases,
        compiler_params=pltpu.CompilerParams(vmem_limit_bytes=VMEM),
        cost_estimate=pl.CostEstimate(
            flops=8 * (group + 1) * size * size * depth * ROOT,
            bytes_accessed=4 * (group + 2) * size * depth * ROOT,
            transcendentals=0,
        ),
        name="correlate",
    )(me, *operands)


def assemble_kernel(groups, *refs):
    sums, (order_ref, out_ref) = refs[:groups], refs[groups:]
    share, width = sums[0].shape[1], sums[0].shape[2] // 2
    for part in range(2):
        lanes = slice(part * width, (part + 1) * width)
        rows = []
        for a in range(groups):
            row = [
                sums[b][a, :, lanes] if a <= b else sums[a][a + 1 + b, :, lanes]
                for b in range(groups)
            ]
            rows.append(jnp.concatenate(row, axis=1))
        placed = jnp.dot(
            jnp.concatenate(rows, axis=0), order_ref[...], preferred_element_type=jnp.float32
        )
        columns = pl.ds(part * width * groups, width * groups)
        for a in range(groups):
            for c in range(share // GROUP):
                first = a * share + c * GROUP
                out_ref[pl.ds((c * groups + a) * GROUP, GROUP), columns] = placed[
                    first : first + GROUP
                ]


def assemble(sums):
    groups = len(sums)
    share, width = sums[0].shape[1], sums[0].shape[2] // 2
    index = np.arange(groups * width).reshape(groups, width // GROUP, GROUP)
    order = np.zeros((groups * width,) * 2, np.float32)
    order[index.transpose(1, 0, 2).reshape(-1), np.arange(groups * width)] = 1.0
    return pl.pallas_call(
        functools.partial(assemble_kernel, groups),
        out_shape=jax.ShapeDtypeStruct((groups * share, 2 * groups * width), jnp.float32),
        compiler_params=pltpu.CompilerParams(vmem_limit_bytes=VMEM),
        name="assemble",
    )(*sums, jnp.asarray(order, jnp.bfloat16))


def body(samples, filter_taps):
    inputs, _, number, _ = samples.shape
    bins = lax.axis_size("chan")
    owners = lax.axis_size("tm")
    per = ROOT // bins
    groups = inputs // GROUP
    me = lax.axis_index("chan").astype(jnp.int32)[None]
    samples = samples.reshape(inputs, 2, number, ROOT, ROOT).transpose(0, 1, 3, 2, 4)
    samples = samples.reshape(inputs, 2, ROOT * number, ROOT)
    matrix, twiddle = tables()
    taps = filter_taps.reshape(TAPS, ROOT, ROOT)
    factor = 1.0 / (number * owners * per * ROOT)
    onward = [(i, i + 1) for i in range(owners - 1)]

    pasts = []

    def fetch(token):
        m = len(pasts)
        if m < groups:
            source = samples
            if token is not None:
                source, _ = lax.optimization_barrier((samples, token))
            pasts.append(lax.ppermute(source[m * GROUP : (m + 1) * GROUP], "tm", onward))

    fetch(None)
    fetch(pasts[0])
    kept = None
    sums = []
    ready = [me] * (groups + 2)

    def lines_of(m):
        return channelize(ready[m], samples, m, pasts[m], bins, taps, matrix, twiddle)

    spectra = lines_of(0)
    fetch(spectra[0])
    for m in range(groups):
        came = {}
        following = None
        for step in range(bins - 1, 0, -1):
            sent = spectra[step]
            if step == min(2, bins - 1) and m + 1 < groups:
                following = lines_of(m + 1)
            if step <= 2 and following is not None:
                sent, _ = lax.optimization_barrier((sent, following[0]))
            came[step] = lax.ppermute(sent, "chan", [(i, i ^ step) for i in range(bins)])
            if step == bins - 1:
                fetch(came[step])
        blocks = [spectra[0]] + [came[step] for step in range(bins - 1, 0, -1)]
        kept, tiles = correlate(me, blocks, kept, m, groups, owners, factor)
        tiles, ready[m + 2] = lax.optimization_barrier((tiles, me))
        sums.append(lax.psum_scatter(tiles, "tm", scatter_dimension=0, tiled=False))
        spectra = following
    return assemble(sums)[None]


def solution(mesh):
    placed = (P("chan", None, "tm", None), P())
    return jax.shard_map(
        body, mesh=mesh, in_specs=placed, out_specs=P("chan", "tm", None), check_vma=False
    )
```

```python
import functools
import math

import jax
import jax.numpy as jnp
import numpy as np
from jax import lax
from jax.experimental import pallas as pl
from jax.experimental.pallas import tpu as pltpu
from jax.sharding import PartitionSpec as P

ROOT = 128
TAPS = 4
GROUP = 16
TILE = 16
AHEAD = 2
VMEM = 56 * 1024 * 1024


def tables():
    indices = np.arange(ROOT)
    product = np.outer(indices, indices)
    angles = (product % ROOT) * (2.0 * math.pi / ROOT)
    cosine, sine = np.cos(angles), np.sin(angles)
    matrix = np.block([[cosine, sine], [-sine, cosine]])
    angles = (product % ROOT**2) * (2.0 * math.pi / ROOT**2)
    twiddle = np.stack([np.cos(angles), np.sin(angles)]) / ROOT
    return jnp.asarray(matrix, jnp.bfloat16), jnp.asarray(twiddle, jnp.float32)


def dot_nt(rows, cols):
    return lax.dot_general(
        rows, cols, (((1,), (1,)), ((), ())), preferred_element_type=jnp.float32
    )


def channelize_one(number, which, own_ref, past_ref, taps_ref, matrix_ref, twiddle_ref,
                   frames, filtered, lines):
    for part in range(2):
        for side, ref in enumerate((past_ref, own_ref)):
            frames[part, side] = ref[part].astype(jnp.float32)

    for first in range(0, ROOT, TILE):
        taps = [taps_ref[tap, pl.ds(first, TILE), :] for tap in range(TAPS)]
        for part in range(2):
            held = [
                frames[
                    part, f // number, pl.ds(first * number + f % number, TILE, stride=number), :
                ]
                for f in range(number - TAPS + 1, 2 * number)
            ]
            for s in range(number):
                total = taps[0] * held[s]
                for tap in range(1, TAPS):
                    total = total + taps[tap] * held[s + tap]
                filtered[pl.ds(part * ROOT + first, TILE), pl.ds(s * ROOT, ROOT)] = total.astype(
                    jnp.bfloat16
                )

    first_pass = jnp.dot(matrix_ref[...], filtered[...], preferred_element_type=jnp.float32)
    cosine, sine = twiddle_ref[0], twiddle_ref[1]
    twisted = []
    for s in range(number):
        real = first_pass[:ROOT, s * ROOT : (s + 1) * ROOT]
        imag = first_pass[ROOT:, s * ROOT : (s + 1) * ROOT]
        twisted.append(
            jnp.concatenate(
                [real * cosine + imag * sine, imag * cosine - real * sine], axis=1
            ).astype(jnp.bfloat16)
        )
    spectra = dot_nt(matrix_ref[...], jnp.concatenate(twisted, axis=0))
    for s in range(number):
        lines[pl.ds(s * 2 * ROOT * GROUP + which, 2 * ROOT, stride=GROUP), :] = spectra[
            :, s * ROOT : (s + 1) * ROOT
        ]


def channelize_kernel(number, bins, me_ref, own_ref, past_ref, taps_ref, matrix_ref, twiddle_ref,
                      *refs):
    out_refs, (frames, filtered, lines) = refs[:bins], refs[bins:]
    per = ROOT // bins
    step = pl.program_id(0)
    for one in range(AHEAD):
        channelize_one(
            number, step * AHEAD + one, own_ref.at[one], past_ref.at[one], taps_ref, matrix_ref,
            twiddle_ref, frames.at[one], filtered.at[one], lines,
        )

    @pl.when(step == pl.num_programs(0) - 1)
    def _():
        for k in range(bins):
            first = pl.multiple_of((me_ref[0] ^ k) * (per * GROUP), GROUP)
            for s in range(number):
                for part in range(2):
                    rows = pl.ds(first + (s * 2 + part) * ROOT * GROUP, per * GROUP)
                    out_refs[k][0, part, s * per : (s + 1) * per] = (
                        lines[rows, :].astype(jnp.bfloat16).reshape(per, GROUP, ROOT)
                    )


def channelize(me, samples, group, past, bins, taps, matrix, twiddle):
    number = samples.shape[2] // ROOT
    per = ROOT // bins
    work = GROUP * 2 * number * ROOT * ROOT
    block = (1, 2, number * per, GROUP, ROOT)
    return pl.pallas_call(
        functools.partial(channelize_kernel, number, bins),
        grid_spec=pltpu.PrefetchScalarGridSpec(
            num_scalar_prefetch=1,
            grid=(GROUP // AHEAD,),
            in_specs=[
                pl.BlockSpec(
                    (AHEAD, 2, ROOT * number, ROOT),
                    lambda i, me: (group * GROUP // AHEAD + i, 0, 0, 0),
                ),
                pl.BlockSpec(
                    (AHEAD, 2, ROOT * number, ROOT), lambda i, me: (i, 0, 0, 0)
                ),
                pl.BlockSpec((TAPS, ROOT, ROOT), lambda i, me: (0, 0, 0)),
                pl.BlockSpec((2 * ROOT, 2 * ROOT), lambda i, me: (0, 0)),
                pl.BlockSpec((2, ROOT, ROOT), lambda i, me: (0, 0, 0)),
            ],
            out_specs=[pl.BlockSpec(block, lambda i, me: (0, 0, 0, 0, 0))] * bins,
            scratch_shapes=[
                pltpu.VMEM((AHEAD, 2, 2, ROOT * number, ROOT), jnp.float32),
                pltpu.VMEM((AHEAD, 2 * ROOT, number * ROOT), jnp.bfloat16),
                pltpu.VMEM((number * 2 * ROOT * GROUP, ROOT), jnp.float32),
            ],
        ),
        out_shape=[jax.ShapeDtypeStruct(block, jnp.bfloat16)] * bins,
        compiler_params=pltpu.CompilerParams(vmem_limit_bytes=VMEM),
        cost_estimate=pl.CostEstimate(
            flops=40 * ROOT * work, bytes_accessed=6 * work, transcendentals=0
        ),
        name="channelize",
    )(me, samples, past, taps, matrix, twiddle)


def correlate_kernel(bins, group, owners, factor, steps, me_ref, *refs):
    blocks, refs = refs[:bins], refs[bins:]
    if group:
        earlier_ref, refs = refs[0], refs[1:]
    kept_ref, out_ref, total = refs
    size = bins * GROUP
    deep = kept_ref.shape[1]
    step = pl.program_id(0)
    for k in range(bins):
        source = me_ref[0] ^ (bins - k if k else 0)
        kept_ref[:, :, pl.ds(pl.multiple_of(source * GROUP, GROUP), GROUP), :] = blocks[k][0]

    real, imag, negated = [], [], []
    for t in range(deep):
        a, b = kept_ref[0, t], kept_ref[1, t]
        real.append(jnp.concatenate([a, b], axis=1))
        imag.append(jnp.concatenate([-b, a], axis=1))
    here = jnp.concatenate(real, axis=1)
    cols = jnp.concatenate([here, jnp.concatenate(imag, axis=1)], axis=0)

    rows = here
    if group:
        earlier = [earlier_ref[part, t] for t in range(deep) for part in range(2)]
        rows = jnp.concatenate([jnp.concatenate(earlier, axis=1), here], axis=0)
    product = dot_nt(rows, cols)

    @pl.when(step == 0)
    def _():
        total[...] = product

    @pl.when(step > 0)
    def _():
        total[...] += product

    @pl.when(step == steps - 1)
    def _():
        share = size // owners
        for n in range(group + 1):
            tile = total[pl.ds(n * size, size), :] * factor
            for t in range(owners):
                out_ref[t, n] = tile[t * share : (t + 1) * share].astype(jnp.bfloat16)
            if n < group:
                mirror = jnp.concatenate([tile[:, :size].T, -tile[:, size:].T], axis=1)
                for t in range(owners):
                    out_ref[t, group + 1 + n] = mirror[t * share : (t + 1) * share].astype(
                        jnp.bfloat16
                    )


def correlate(me, blocks, kept, group, groups, owners, factor):
    bins = len(blocks)
    depth = blocks[0].shape[2]
    size = bins * GROUP
    deep = max(1, depth // 8)
    steps = depth // deep
    block_spec = pl.BlockSpec((1, 2, deep, GROUP, ROOT), lambda k, me: (0, 0, k, 0, 0))
    kept_shape = jax.ShapeDtypeStruct((2, depth, groups * size, ROOT), jnp.bfloat16)
    out_shape = jax.ShapeDtypeStruct(
        (owners, 2 * group + 1, size // owners, 2 * size), jnp.bfloat16
    )
    in_specs = [block_spec] * bins
    operands = list(blocks)
    aliases = {}
    if group:
        in_specs.append(
            pl.BlockSpec((2, deep, group * size, ROOT), lambda k, me: (0, k, 0, 0))
        )
        operands.append(kept)
        aliases = {1 + bins: 0}
    return pl.pallas_call(
        functools.partial(correlate_kernel, bins, group, owners, factor, steps),
        grid_spec=pltpu.PrefetchScalarGridSpec(
            num_scalar_prefetch=1,
            grid=(steps,),
            in_specs=in_specs,
            out_specs=[
                pl.BlockSpec((2, deep, size, ROOT), lambda k, me: (0, k, group, 0)),
                pl.BlockSpec(out_shape.shape, lambda k, me: (0, 0, 0, 0)),
            ],
            scratch_shapes=[pltpu.VMEM(((group + 1) * size, 2 * size), jnp.float32)],
        ),
        out_shape=[kept_shape, out_shape],
        input_output_aliases=aliases,
        compiler_params=pltpu.CompilerParams(vmem_limit_bytes=VMEM),
        cost_estimate=pl.CostEstimate(
            flops=8 * (group + 1) * size * size * depth * ROOT,
            bytes_accessed=4 * (group + 2) * size * depth * ROOT,
            transcendentals=0,
        ),
        name="correlate",
    )(me, *operands)


def assemble_kernel(groups, *refs):
    sums, shares, (order_ref, out_ref) = refs[: groups - 1], refs[groups - 1 : -2], refs[-2:]
    last = shares[0][0].astype(jnp.float32)
    for ref in shares[1:]:
        last = last + ref[0].astype(jnp.float32)
    sums = (*sums, last.astype(jnp.bfloat16))
    share, width = last.shape[1], last.shape[2] // 2
    for part in range(2):
        lanes = slice(part * width, (part + 1) * width)
        rows = []
        for a in range(groups):
            row = [
                sums[b][a, :, lanes] if a <= b else sums[a][a + 1 + b, :, lanes]
                for b in range(groups)
            ]
            rows.append(jnp.concatenate(row, axis=1))
        placed = jnp.dot(
            jnp.concatenate(rows, axis=0), order_ref[...], preferred_element_type=jnp.float32
        )
        columns = pl.ds(part * width * groups, width * groups)
        for a in range(groups):
            for c in range(share // GROUP):
                first = a * share + c * GROUP
                out_ref[pl.ds((c * groups + a) * GROUP, GROUP), columns] = placed[
                    first : first + GROUP
                ]


def assemble(sums, shares):
    groups = len(sums) + 1
    share, width = shares[0].shape[2], shares[0].shape[3] // 2
    index = np.arange(groups * width).reshape(groups, width // GROUP, GROUP)
    order = np.zeros((groups * width,) * 2, np.float32)
    order[index.transpose(1, 0, 2).reshape(-1), np.arange(groups * width)] = 1.0
    return pl.pallas_call(
        functools.partial(assemble_kernel, groups),
        out_shape=jax.ShapeDtypeStruct((groups * share, 2 * groups * width), jnp.float32),
        compiler_params=pltpu.CompilerParams(vmem_limit_bytes=VMEM),
        name="assemble",
    )(*sums, *shares, jnp.asarray(order, jnp.bfloat16))


def body(samples, filter_taps):
    inputs, _, number, _ = samples.shape
    bins = lax.axis_size("chan")
    owners = lax.axis_size("tm")
    per = ROOT // bins
    groups = inputs // GROUP
    me = lax.axis_index("chan").astype(jnp.int32)[None]
    samples = samples.reshape(inputs, 2, number, ROOT, ROOT).transpose(0, 1, 3, 2, 4)
    samples = samples.reshape(inputs, 2, ROOT * number, ROOT)
    matrix, twiddle = tables()
    taps = filter_taps.reshape(TAPS, ROOT, ROOT)
    factor = 1.0 / (number * owners * per * ROOT)
    onward = [(i, i + 1) for i in range(owners - 1)]

    pasts = []

    def fetch(token):
        m = len(pasts)
        if m < groups:
            source = samples
            if token is not None:
                source, _ = lax.optimization_barrier((samples, token))
            pasts.append(lax.ppermute(source[m * GROUP : (m + 1) * GROUP], "tm", onward))

    fetch(None)
    kept = None
    sums = []
    held = None
    ready = [me] * (groups + 2)

    def lines_of(m):
        return channelize(ready[m], samples, m, pasts[m], bins, taps, matrix, twiddle)

    spectra = lines_of(0)
    fetch(spectra[0])
    fetch(spectra[0])
    for m in range(groups):
        came = {}
        following = None
        for step in range(bins - 1, 0, -1):
            sent = spectra[step]
            if step == min(2, bins - 1) and m + 1 < groups:
                following = lines_of(m + 1)
            if step <= 2 and following is not None:
                sent, _ = lax.optimization_barrier((sent, following[0]))
            came[step] = lax.ppermute(sent, "chan", [(i, i ^ step) for i in range(bins)])
            if step == bins - 1:
                fetch(came[step])
        blocks = [spectra[0]] + [came[step] for step in range(bins - 1, 0, -1)]
        spectra = following
        if m == groups - 2:
            held = blocks
            continue
        if held is not None:
            held[0], _ = lax.optimization_barrier((held[0], came[bins - 1]))
            kept, tiles = correlate(me, held, kept, m - 1, groups, owners, factor)
            sums.append(lax.psum_scatter(tiles, "tm", scatter_dimension=0, tiled=False))
        kept, tiles = correlate(me, blocks, kept, m, groups, owners, factor)
        if m < groups - 1:
            tiles, ready[m + 2] = lax.optimization_barrier((tiles, me))
            sums.append(lax.psum_scatter(tiles, "tm", scatter_dimension=0, tiled=False))
    here = lax.axis_index("tm")
    shares = [lax.dynamic_slice_in_dim(tiles, here, 1, 0)]
    for step in range(1, owners):
        sent = lax.dynamic_slice_in_dim(tiles, here ^ step, 1, 0)
        shares.append(lax.ppermute(sent, "tm", [(i, i ^ step) for i in range(owners)]))
    return assemble(sums, shares)[None]


def solution(mesh):
    placed = (P("chan", None, "tm", None), P())
    return jax.shard_map(
        body, mesh=mesh, in_specs=placed, out_specs=P("chan", "tm", None), check_vma=False
    )
```

```python
import functools
import math

import jax
import jax.numpy as jnp
import numpy as np
from jax import lax
from jax.experimental import pallas as pl
from jax.experimental.pallas import tpu as pltpu
from jax.sharding import PartitionSpec as P

ROOT = 128
TAPS = 4
GROUP = 16
TILE = 16
AHEAD = 2
LATE = 3
VMEM = 56 * 1024 * 1024


def tables():
    indices = np.arange(ROOT)
    product = np.outer(indices, indices)
    angles = (product % ROOT) * (2.0 * math.pi / ROOT)
    cosine, sine = np.cos(angles), np.sin(angles)
    matrix = np.block([[cosine, sine], [-sine, cosine]])
    angles = (product % ROOT**2) * (2.0 * math.pi / ROOT**2)
    twiddle = np.stack([np.cos(angles), np.sin(angles)]) / ROOT
    return jnp.asarray(matrix, jnp.bfloat16), jnp.asarray(twiddle, jnp.float32)


def dot_nt(rows, cols):
    return lax.dot_general(
        rows, cols, (((1,), (1,)), ((), ())), preferred_element_type=jnp.float32
    )


def channelize_one(number, which, own_ref, past_ref, taps_ref, matrix_ref, twiddle_ref,
                   frames, filtered, lines):
    for part in range(2):
        for side, ref in enumerate((past_ref, own_ref)):
            frames[part, side] = ref[part].astype(jnp.float32)

    for first in range(0, ROOT, TILE):
        taps = [taps_ref[tap, pl.ds(first, TILE), :] for tap in range(TAPS)]
        for part in range(2):
            held = [
                frames[
                    part, f // number, pl.ds(first * number + f % number, TILE, stride=number), :
                ]
                for f in range(number - TAPS + 1, 2 * number)
            ]
            for s in range(number):
                total = taps[0] * held[s]
                for tap in range(1, TAPS):
                    total = total + taps[tap] * held[s + tap]
                filtered[pl.ds(part * ROOT + first, TILE), pl.ds(s * ROOT, ROOT)] = total.astype(
                    jnp.bfloat16
                )

    first_pass = jnp.dot(matrix_ref[...], filtered[...], preferred_element_type=jnp.float32)
    cosine, sine = twiddle_ref[0], twiddle_ref[1]
    twisted = []
    for s in range(number):
        real = first_pass[:ROOT, s * ROOT : (s + 1) * ROOT]
        imag = first_pass[ROOT:, s * ROOT : (s + 1) * ROOT]
        twisted.append(
            jnp.concatenate(
                [real * cosine + imag * sine, imag * cosine - real * sine], axis=1
            ).astype(jnp.bfloat16)
        )
    spectra = dot_nt(matrix_ref[...], jnp.concatenate(twisted, axis=0))
    for s in range(number):
        lines[pl.ds(s * 2 * ROOT * GROUP + which, 2 * ROOT, stride=GROUP), :] = spectra[
            :, s * ROOT : (s + 1) * ROOT
        ]


def channelize_kernel(number, bins, me_ref, own_ref, past_ref, taps_ref, matrix_ref, twiddle_ref,
                      *refs):
    out_refs, (frames, filtered, lines) = refs[:bins], refs[bins:]
    per = ROOT // bins
    step = pl.program_id(0)
    for one in range(AHEAD):
        channelize_one(
            number, step * AHEAD + one, own_ref.at[one], past_ref.at[one], taps_ref, matrix_ref,
            twiddle_ref, frames.at[one], filtered.at[one], lines,
        )

    @pl.when(step == pl.num_programs(0) - 1)
    def _():
        for k in range(bins):
            first = pl.multiple_of((me_ref[0] ^ k) * (per * GROUP), GROUP)
            for s in range(number):
                for part in range(2):
                    rows = pl.ds(first + (s * 2 + part) * ROOT * GROUP, per * GROUP)
                    out_refs[k][0, part, s * per : (s + 1) * per] = (
                        lines[rows, :].astype(jnp.bfloat16).reshape(per, GROUP, ROOT)
                    )


def send_order(bins):
    far, near = range(bins - 1, bins // 2 - 1, -1), range(bins // 2 - 1, 0, -1)
    steps = [far[0]]
    for pair in zip(near, far[1:]):
        steps.extend(pair)
    return steps


def channelize(me, samples, group, past, bins, taps, matrix, twiddle):
    number = samples.shape[2] // ROOT
    per = ROOT // bins
    work = GROUP * 2 * number * ROOT * ROOT
    block = (1, 2, number * per, GROUP, ROOT)
    return pl.pallas_call(
        functools.partial(channelize_kernel, number, bins),
        grid_spec=pltpu.PrefetchScalarGridSpec(
            num_scalar_prefetch=1,
            grid=(GROUP // AHEAD,),
            in_specs=[
                pl.BlockSpec(
                    (AHEAD, 2, ROOT * number, ROOT),
                    lambda i, me: (group * GROUP // AHEAD + i, 0, 0, 0),
                ),
                pl.BlockSpec(
                    (AHEAD, 2, ROOT * number, ROOT), lambda i, me: (i, 0, 0, 0)
                ),
                pl.BlockSpec((TAPS, ROOT, ROOT), lambda i, me: (0, 0, 0)),
                pl.BlockSpec((2 * ROOT, 2 * ROOT), lambda i, me: (0, 0)),
                pl.BlockSpec((2, ROOT, ROOT), lambda i, me: (0, 0, 0)),
            ],
            out_specs=[pl.BlockSpec(block, lambda i, me: (0, 0, 0, 0, 0))] * bins,
            scratch_shapes=[
                pltpu.VMEM((AHEAD, 2, 2, ROOT * number, ROOT), jnp.float32),
                pltpu.VMEM((AHEAD, 2 * ROOT, number * ROOT), jnp.bfloat16),
                pltpu.VMEM((number * 2 * ROOT * GROUP, ROOT), jnp.float32),
            ],
        ),
        out_shape=[jax.ShapeDtypeStruct(block, jnp.bfloat16)] * bins,
        compiler_params=pltpu.CompilerParams(vmem_limit_bytes=VMEM),
        cost_estimate=pl.CostEstimate(
            flops=40 * ROOT * work, bytes_accessed=6 * work, transcendentals=0
        ),
        name="channelize",
    )(me, samples, past, taps, matrix, twiddle)


def correlate_kernel(bins, group, groups, owners, factor, steps, me_ref, *refs):
    blocks, refs = refs[:bins], refs[bins:]
    if group:
        earlier_ref, refs = refs[0], refs[1:]
    kept_ref, out_ref, total = refs if group < groups - 1 else (refs[2], refs[0], refs[1])
    size = bins * GROUP
    deep = kept_ref.shape[1]
    step = pl.program_id(0)
    for k, partner in enumerate([0, *send_order(bins)]):
        source = me_ref[0] ^ partner
        kept_ref[:, :, pl.ds(pl.multiple_of(source * GROUP, GROUP), GROUP), :] = blocks[k][0]

    real, imag = [], []
    for t in range(deep):
        a, b = kept_ref[0, t], kept_ref[1, t]
        real.append(jnp.concatenate([a, b], axis=1))
        imag.append(jnp.concatenate([-b, a], axis=1))
    here = jnp.concatenate(real, axis=1)
    cols = jnp.concatenate([here, jnp.concatenate(imag, axis=1)], axis=0)

    rows = here
    if group:
        earlier = [earlier_ref[part, t] for t in range(deep) for part in range(2)]
        rows = jnp.concatenate([jnp.concatenate(earlier, axis=1), here], axis=0)
    product = dot_nt(rows, cols)

    @pl.when(step == 0)
    def _():
        total[...] = product

    @pl.when(step > 0)
    def _():
        total[...] += product

    @pl.when(step == steps - 1)
    def _():
        share = size // owners
        for n in range(group + 1):
            tile = total[pl.ds(n * size, size), :] * factor
            for t in range(owners):
                out_ref[t, n] = tile[t * share : (t + 1) * share].astype(jnp.bfloat16)
            if n < group:
                mirror = jnp.concatenate([tile[:, :size].T, -tile[:, size:].T], axis=1)
                for t in range(owners):
                    out_ref[t, group + 1 + n] = mirror[t * share : (t + 1) * share].astype(
                        jnp.bfloat16
                    )


def correlate(me, blocks, kept, group, groups, owners, factor):
    bins = len(blocks)
    depth = blocks[0].shape[2]
    size = bins * GROUP
    deep = max(1, depth // 8)
    steps = depth // deep
    block_spec = pl.BlockSpec((1, 2, deep, GROUP, ROOT), lambda k, me: (0, 0, k, 0, 0))
    kept_shape = jax.ShapeDtypeStruct((2, depth, groups * size, ROOT), jnp.bfloat16)
    out_shape = jax.ShapeDtypeStruct(
        (owners, 2 * group + 1, size // owners, 2 * size), jnp.bfloat16
    )
    in_specs = [block_spec] * bins
    operands = list(blocks)
    aliases = {}
    if group:
        in_specs.append(
            pl.BlockSpec((2, deep, group * size, ROOT), lambda k, me: (0, k, 0, 0))
        )
        operands.append(kept)
        aliases = {1 + bins: 0}
    out_specs = [pl.BlockSpec(out_shape.shape, lambda k, me: (0, 0, 0, 0))]
    out_shapes = [out_shape]
    scratch = [pltpu.VMEM(((group + 1) * size, 2 * size), jnp.float32)]
    kept_block = (2, deep, size, ROOT)
    if group < groups - 1:
        out_specs.insert(0, pl.BlockSpec(kept_block, lambda k, me: (0, k, group, 0)))
        out_shapes.insert(0, kept_shape)
    else:
        scratch.append(pltpu.VMEM(kept_block, jnp.bfloat16))
        aliases = {}
    return pl.pallas_call(
        functools.partial(correlate_kernel, bins, group, groups, owners, factor, steps),
        grid_spec=pltpu.PrefetchScalarGridSpec(
            num_scalar_prefetch=1,
            grid=(steps,),
            in_specs=in_specs,
            out_specs=out_specs,
            scratch_shapes=scratch,
        ),
        out_shape=out_shapes,
        input_output_aliases=aliases,
        compiler_params=pltpu.CompilerParams(vmem_limit_bytes=VMEM),
        cost_estimate=pl.CostEstimate(
            flops=8 * (group + 1) * size * size * depth * ROOT,
            bytes_accessed=4 * (group + 2) * size * depth * ROOT,
            transcendentals=0,
        ),
        name="correlate",
    )(me, *operands)


def assemble_kernel(groups, *refs):
    sums, shares, (order_ref, out_ref) = refs[: groups - 1], refs[groups - 1 : -2], refs[-2:]
    last = shares[0][0].astype(jnp.float32)
    for ref in shares[1:]:
        last = last + ref[0].astype(jnp.float32)
    sums = (*sums, last.astype(jnp.bfloat16))
    share, width = last.shape[1], last.shape[2] // 2
    for part in range(2):
        lanes = slice(part * width, (part + 1) * width)
        rows = []
        for a in range(groups):
            row = [
                sums[b][a, :, lanes] if a <= b else sums[a][a + 1 + b, :, lanes]
                for b in range(groups)
            ]
            rows.append(jnp.concatenate(row, axis=1))
        placed = jnp.dot(
            jnp.concatenate(rows, axis=0), order_ref[...], preferred_element_type=jnp.float32
        )
        columns = pl.ds(part * width * groups, width * groups)
        for a in range(groups):
            for c in range(share // GROUP):
                first = a * share + c * GROUP
                out_ref[pl.ds((c * groups + a) * GROUP, GROUP), columns] = placed[
                    first : first + GROUP
                ]


def assemble(sums, shares):
    groups = len(sums) + 1
    share, width = shares[0].shape[2], shares[0].shape[3] // 2
    index = np.arange(groups * width).reshape(groups, width // GROUP, GROUP)
    order = np.zeros((groups * width,) * 2, np.float32)
    order[index.transpose(1, 0, 2).reshape(-1), np.arange(groups * width)] = 1.0
    return pl.pallas_call(
        functools.partial(assemble_kernel, groups),
        out_shape=jax.ShapeDtypeStruct((groups * share, 2 * groups * width), jnp.float32),
        compiler_params=pltpu.CompilerParams(vmem_limit_bytes=VMEM),
        name="assemble",
    )(*sums, *shares, jnp.asarray(order, jnp.bfloat16))


def body(samples, filter_taps):
    inputs, _, number, _ = samples.shape
    bins = lax.axis_size("chan")
    owners = lax.axis_size("tm")
    per = ROOT // bins
    groups = inputs // GROUP
    me = lax.axis_index("chan").astype(jnp.int32)[None]
    samples = samples.reshape(inputs, 2, number, ROOT, ROOT).transpose(0, 1, 3, 2, 4)
    samples = samples.reshape(inputs, 2, ROOT * number, ROOT)
    matrix, twiddle = tables()
    taps = filter_taps.reshape(TAPS, ROOT, ROOT)
    factor = 1.0 / (number * owners * per * ROOT)
    onward = [(i, i + 1) for i in range(owners - 1)]

    pasts = []

    def fetch(token):
        m = len(pasts)
        if m < groups:
            source = samples
            if token is not None:
                source, _ = lax.optimization_barrier((samples, token))
            sent = source[m * GROUP : (m + 1) * GROUP]
            pasts.append(lax.ppermute(sent, "tm", onward))
            return sent

    sent = None
    for _ in range(3):
        sent = fetch(sent)
    order = send_order(bins)
    kept = None
    sums = []
    held = None
    ready = [me] * (groups + 2)

    def lines_of(m):
        return channelize(ready[m], samples, m, pasts[m], bins, taps, matrix, twiddle)

    spectra = lines_of(0)
    for m in range(groups):
        came = []
        following = None
        for place, step in enumerate(order):
            sent = spectra[step]
            if place == max(bins - LATE, 0) and m + 1 < groups:
                following = lines_of(m + 1)
            if following is not None:
                sent, _ = lax.optimization_barrier((sent, following[0]))
            came.append(lax.ppermute(sent, "chan", [(i, i ^ step) for i in range(bins)]))
            if place == 0:
                fetch(came[0])
        blocks = [spectra[0]] + came
        spectra = following
        if m == groups - 2:
            held = blocks
            continue
        if held is not None:
            held[0], _ = lax.optimization_barrier((held[0], came[0]))
            kept, tiles = correlate(me, held, kept, m - 1, groups, owners, factor)
            sums.append(lax.psum_scatter(tiles, "tm", scatter_dimension=0, tiled=False))
        *kept_after, tiles = correlate(me, blocks, kept, m, groups, owners, factor)
        if m < groups - 1:
            (kept,) = kept_after
            tiles, ready[m + 2] = lax.optimization_barrier((tiles, me))
            sums.append(lax.psum_scatter(tiles, "tm", scatter_dimension=0, tiled=False))
    here = lax.axis_index("tm")
    shares = [lax.dynamic_slice_in_dim(tiles, here, 1, 0)]
    for step in range(1, owners):
        sent = lax.dynamic_slice_in_dim(tiles, here ^ step, 1, 0)
        shares.append(lax.ppermute(sent, "tm", [(i, i ^ step) for i in range(owners)]))
    return assemble(sums, shares)[None]


def solution(mesh):
    placed = (P("chan", None, "tm", None), P())
    return jax.shard_map(
        body, mesh=mesh, in_specs=placed, out_specs=P("chan", "tm", None), check_vma=False
    )
```
